256 devices in a mesh: section: 4 (over y_lo, core), fsdp: 64 (over z, x, y_hi).
Axes of the slice: x: 4, y: 4 (y_hi: 2, y_lo: 2; y = y_hi * 2 + y_lo), z: 8, core: 2. Of those that a mesh axis runs over, the one named last changes fastest.
Arguments:
- hidden: bfloat16 [1024, 4608], P('section', 'fsdp'), may hold values from -6 to 6
- embedding: bfloat16 [128000, 4608], P('fsdp', 'section'), may hold values from -0.1875 to 0.1875
- targets: int32 [1024], P('section'), may hold values from 0 to 127999
- input_grad: bfloat16 [8192, 4608], P('fsdp', 'section'), as said below
- first_moment: float32 [8192, 4608], P('fsdp', 'section')
- second_moment: float32 [8192, 4608], P('fsdp', 'section'), as said below
- exponents: int32 [8192, 36], P('fsdp', 'section'), may hold values from -13 to -4
Outputs:
- hidden_grad: bfloat16 [1024, 4608], P('section', 'fsdp')
- new_embedding: bfloat16 [8192, 4608], P('fsdp')
- new_first: float32 [8192, 4608], P('fsdp', 'section')
- new_second: float32 [8192, 4608], P('fsdp', 'section')
- scaled_table: bfloat16 [8192, 4608], P('fsdp', 'section')
The draws below stay inside these ranges and needn't reach their ends.
Inputs may be any that keep to these rules, and one draw needn't show every extreme that they name: `input_grad`: a row of the window is zero unless one or more of 1024 input token ids of the microbatch name it. `second_moment`: entries are positive.
All inputs are finite; a program needn't handle non-finite values.
Results may differ from the reference program's by a relative error of at most 0.0044.
Values may be sent and summed in bfloat16 or wider, within the bound.
No kernel may reach another device: no remote copies, remote signals or barrier semaphores. Data moves between devices by JAX's collectives and lax.ppermute only.
A program may use at most 128 MiB of HBM per device.

```python
import math
import jax
import jax.numpy as jnp
from jax import lax

D = 4608
VOC_DEV = 2000
UPD_DEV = 128
BLOCK = 128
VOCAB = 128000
WINDOW = 8192
TOKENS = 1024
N_FSDP = 64


def moment_scale():
    return 2.0 * math.sqrt(TOKENS) / VOCAB


def draw_input_grad(key, part):
    key = jax.random.fold_in(key, 7)
    key_ids = jax.random.fold_in(key, 1)
    key_vals = jax.random.fold_in(key, 2)
    input_ids = jax.random.randint(key_ids, (TOKENS,), 0, VOCAB, dtype=jnp.int32)
    rows = jnp.arange(WINDOW, dtype=jnp.int32)
    row_ids = rows // UPD_DEV * VOC_DEV + rows % UPD_DEV
    counts = jnp.sum((row_ids[:, None] == input_ids[None, :]).astype(jnp.float32), axis=1)
    values = jnp.clip(jax.random.normal(key_vals, (WINDOW, D), jnp.float32), -4.0, 4.0)
    result = values * jnp.sqrt(counts)[:, None] * moment_scale()
    return result.astype(jnp.bfloat16)


def draw_first_moment(key, part):
    key = jax.random.fold_in(key, 11)
    key_vals = jax.random.fold_in(key, 1)
    values = jnp.clip(jax.random.normal(key_vals, (WINDOW, D), jnp.float32), -4.0, 4.0)
    return (values * (moment_scale() / 3.0)).astype(jnp.float32)


def draw_second_moment(key, part):
    key = jax.random.fold_in(key, 13)
    logs = jax.random.uniform(key, (WINDOW, D), jnp.float32, math.log(0.02), math.log(0.2))
    base = moment_scale()
    return (jnp.exp(logs) * (base * base)).astype(jnp.float32)


def plant(drawn, stream_key, least, top_value):
    shape = drawn.shape
    index_at = [jax.random.randint(jax.random.fold_in(stream_key, axis), (), 0, shape[axis]) for axis in range(len(shape))]
    drawn = drawn.at[tuple(index_at)].set(least)
    longest = shape.index(max(shape))
    index_at[longest] = (index_at[longest] + 1) % shape[longest]
    return drawn.at[tuple(index_at)].set(top_value)


def shard_levels(own_key, dims, split, low, high):
    level, own = 1.0, jax.random.fold_in(own_key, 6)
    for dim, shards_of in split:
        heights = jnp.exp(jax.random.uniform(jax.random.fold_in(own, dim), (shards_of,), jnp.float32, low / len(split), high / len(split)))
        level = level * jnp.repeat(heights, dims[dim] // shards_of).reshape([-1 if axis == dim else 1 for axis in range(len(dims))])
    return level


def bell_draw(rng, extent, scale, reach, shards=(), kind=jnp.bfloat16):
    array = scale * jax.random.normal(rng, extent, jnp.float32)
    if shards:
        array = array * shard_levels(rng, extent, shards, -0.22, 0.18)
    return jnp.clip(array, -reach, reach).astype(kind)


def setup_inputs(seed: int = 0) -> dict:
    seeds = jax.random.split(jax.random.key(seed), 8)
    hidden = bell_draw(seeds[0], (TOKENS, D), 1.0, 6.0, ((0, 4), (1, 64)))
    embedding = bell_draw(seeds[1], (VOCAB, D), (D // 4) ** -0.5, 0.1875, ((0, 64), (1, 4)))
    targets = plant(jax.random.randint(seeds[2], (TOKENS,), 0, VOCAB), jax.random.fold_in(seeds[2], 1), 0, VOCAB - 1).astype(jnp.int32)
    input_grad = draw_input_grad(jax.random.fold_in(seeds[7], 71), 0)
    first_moment = draw_first_moment(jax.random.fold_in(seeds[7], 71), 0)
    second_moment = draw_second_moment(jax.random.fold_in(seeds[7], 71), 0)
    exponents = plant(jax.random.randint(seeds[6], (WINDOW, D // BLOCK), -13, -3), jax.random.fold_in(seeds[6], 1), -13, (-3) - 1).astype(jnp.int32)
    return dict(hidden=hidden, embedding=embedding, targets=targets, input_grad=input_grad, first_moment=first_moment, second_moment=second_moment, exponents=exponents)


softcap = 30.0
learn_rate = 0.01
beta_one = 0.9
beta_two = 0.95
adam_step = 100.0
epsilon = 1e-08

def power_two(shifts):
    result = jnp.ones(shifts.shape, jnp.float32)
    for bit in range(4):
        factor = float(2 ** 2 ** bit)
        result = result * jnp.where(shifts >> bit & 1 == 1, factor, 1.0).astype(jnp.float32)
    return result

def reference(hidden, embedding, targets, input_grad, first_moment, second_moment, exponents):
    raw_logits = jnp.dot(hidden, embedding.T, preferred_element_type=jnp.float32)
    capped = softcap * jnp.tanh(raw_logits / softcap)
    weights = jnp.exp(capped)
    totals = lax.optimization_barrier(jnp.sum(weights, axis=1, keepdims=True))
    vocab_ids = jnp.arange(VOCAB, dtype=jnp.int32)
    onehot = (targets[:, None] == vocab_ids[None, :]).astype(jnp.float32)
    ratio = capped / softcap
    slopes = 1.0 - ratio * ratio
    logit_grad = ((weights / totals - onehot) * slopes).astype(jnp.bfloat16)
    hidden_grad = jnp.dot(logit_grad, embedding, preferred_element_type=jnp.float32).astype(jnp.bfloat16)
    window_grad = logit_grad.reshape(TOKENS, N_FSDP, VOC_DEV)[:, :, :UPD_DEV].reshape(TOKENS, WINDOW)
    old_rows = embedding.reshape(N_FSDP, VOC_DEV, D)[:, :UPD_DEV, :].reshape(WINDOW, D)
    grad = jnp.dot(window_grad.T, hidden, preferred_element_type=jnp.float32) + input_grad.astype(jnp.float32)
    new_first = beta_one * first_moment + (1.0 - beta_one) * grad
    new_second = beta_two * second_moment + (1.0 - beta_two) * grad * grad
    correct_one = 1.0 - beta_one ** adam_step
    correct_two = 1.0 - beta_two ** adam_step
    update = new_first / correct_one / (jnp.sqrt(new_second / correct_two) + epsilon)
    new_embedding = (old_rows.astype(jnp.float32) - learn_rate * update).astype(jnp.bfloat16)
    blocks = exponents.shape[1]
    scaling = power_two(-exponents)
    shaped = new_embedding.astype(jnp.float32).reshape(WINDOW, blocks, BLOCK) * scaling[:, :, None]
    scaled_table = jnp.clip(shaped, -448.0, 448.0).reshape(WINDOW, D).astype(jnp.bfloat16)
    return (hidden_grad, new_embedding, new_first, new_second, scaled_table)
```

```python
import jax
import jax.numpy as jnp
from jax import lax
from jax.sharding import Mesh
from jax.sharding import PartitionSpec as P

BLOCK = 128
AXES = ("yl", "c", "z", "x", "yh")
NZ, NX, NY = 8, 4, 4

softcap = 30.0
learn_rate = 0.01
beta_one = 0.9
beta_two = 0.95
adam_step = 100.0
epsilon = 1e-08
bf16 = jnp.bfloat16
f32 = jnp.float32


def power_two(shifts):
    result = jnp.ones(shifts.shape, f32)
    for bit in range(4):
        factor = float(2**2**bit)
        result = result * jnp.where(shifts >> bit & 1 == 1, factor, 1.0).astype(f32)
    return result


def turn(axis, size, step):
    return axis, [(i, (i + step) % size) for i in range(size)]


def turn_y(step):
    place = lambda y: (y % 2) * 2 + y // 2
    return ("yl", "yh"), [(place(y), place((y + step) % NY)) for y in range(NY)]


def send(value, way):
    axis, pairs = way
    return lax.ppermute(value, axis, pairs)


def gather_ring(block, size, up, down):
    half = block.shape[0] // 2
    found = []
    low, high = block, block
    for step in range(1, size // 2):
        low = send(low, up)
        high = send(high, down)
        found.append((-step, 0, low))
        found.append((step, 0, high))
    low = send(low[:half], up)
    high = send(high[half:], down)
    found.append((size // 2, 0, low))
    found.append((size // 2, half, high))
    return found


def scatter_ring(block, up, down):
    one, two, three = block(1), block(2), block(3)
    half = one.shape[0] // 2
    from_low = send(jnp.concatenate([two[:half], one[half:]]), up)
    from_high = send(jnp.concatenate([two[half:], three[:half]]), down)
    next_up = (one[:half].astype(f32) + from_low[:half].astype(f32)).astype(bf16)
    next_down = (three[half:].astype(f32) + from_high[:half].astype(f32)).astype(bf16)
    last_low = send(next_up, up)
    last_high = send(next_down, down)
    own = block(0).astype(f32)
    low = own[:half] + from_high[half:].astype(f32) + last_low.astype(f32)
    high = own[half:] + from_low[half:].astype(f32) + last_high.astype(f32)
    return jnp.concatenate([low, high])


def local(hidden, embedding, targets, input_grad, first_moment, second_moment, exponents):
    yl, core, z, x, yh = (lax.axis_index(name) for name in AXES)
    section = yl * 2 + core
    fsdp = (z * NX + x) * 2 + yh
    y = yh * 2 + yl
    vocab_rows, quarter = embedding.shape
    rows = vocab_rows // 2
    tokens, width = hidden.shape
    window_rows = input_grad.shape[0]
    lanes = tokens // 2
    swap_y = turn("yl", 2, 1)
    swap_core = turn("c", 2, 1)
    swap_far = turn("yh", 2, 1)
    x_up, x_down = turn("x", NX, 1), turn("x", NX, -1)
    z_up, z_down = turn("z", NZ, 1), turn("z", NZ, -1)
    y_up, y_down = turn_y(1), turn_y(-1)

    table = jnp.zeros((rows, 4 * quarter), bf16)
    mine = lax.dynamic_slice(embedding, (yl * rows, 0), (rows, quarter))
    cuts = [0, 256, 512, 768, rows] if rows > 1000 - 1 else [0, rows // 2, rows]
    pieces = []
    for begin, end in zip(cuts[:-1], cuts[1:]):
        part = lax.dynamic_slice(
            embedding, ((1 - yl) * rows + begin, 0), (end - begin, quarter)
        )
        pieces.append((begin, send(part, swap_y)))
    table = lax.dynamic_update_slice(table, mine, (0, 0))
    table = lax.dynamic_update_slice(table, send(mine, swap_core), (0, quarter))
    for begin, piece in pieces:
        table = lax.dynamic_update_slice(table, piece, (begin, 2 * quarter))
        table = lax.dynamic_update_slice(table, send(piece, swap_core), (begin, 3 * quarter))

    def pair_lanes(own, other):
        first = jnp.where(yl == 0, own, other)
        second = jnp.where(yl == 0, other, own)
        return jnp.concatenate(
            [first[..., :lanes], second[..., :lanes], first[..., lanes:], second[..., lanes:]], axis=-1
        )

    turned = hidden.T
    both = pair_lanes(turned, send(turned, swap_y))
    other_both = send(both, swap_far)
    strip = jnp.concatenate(
        [jnp.where(yh == 0, both, other_both), jnp.where(yh == 0, other_both, both)], axis=0
    )
    strip_a, strip_b = strip[:, :tokens], strip[:, tokens:]
    high = 2 * width
    flip = 2 * section

    across = jnp.zeros((NX, high, tokens), bf16)
    across = lax.dynamic_update_slice(across, strip_a[None], (x, 0, 0))
    for offset, lead, block in gather_ring(strip_a, NX, x_up, x_down):
        across = lax.dynamic_update_slice(across, block[None], ((x + offset) % NX, lead, 0))
    along = jnp.zeros((NZ, high, tokens), bf16)
    along = lax.dynamic_update_slice(along, strip_b[None], (z ^ flip, 0, 0))
    for offset, lead, block in gather_ring(strip_b, NZ, z_up, z_down):
        along = lax.dynamic_update_slice(along, block[None], (((z + offset) % NZ) ^ flip, lead, 0))

    states = jnp.zeros((NZ, NX, high, 2 * tokens), bf16)
    states = lax.dynamic_update_slice(states, across[None], (z ^ flip, 0, 0, 0))
    for offset, lead, block in gather_ring(across, NZ, z_up, z_down):
        states = lax.dynamic_update_slice(
            states, block[None], (((z + offset) % NZ) ^ flip, lead, 0, 0)
        )
    states = lax.dynamic_update_slice(states, along[:, None], (0, x, 0, tokens))
    for offset, lead, block in gather_ring(along, NX, x_up, x_down):
        states = lax.dynamic_update_slice(
            states, block[:, None], (lead, (x + offset) % NX, 0, tokens)
        )
    states = states.reshape(4 * quarter, 2 * tokens)
    goals = pair_lanes(targets, send(targets, swap_y))

    raw_logits = jnp.dot(table, states, preferred_element_type=f32)
    capped = softcap * jnp.tanh(raw_logits / softcap)
    weights = jnp.exp(capped)
    sums = jnp.sum(weights, axis=0).reshape(-1, BLOCK)
    peers = NZ * NX * NY
    everyone = lax.all_to_all(
        jnp.broadcast_to(sums[None], (peers,) + sums.shape), ("yl", "z", "x", "yh"), 0, 0
    )
    totals = jnp.sum(everyone, axis=0).reshape(1, -1)
    vocab_ids = fsdp * vocab_rows + yl * rows + lax.broadcasted_iota(jnp.int32, (rows, 1), 0)
    onehot = (goals[None, :] == vocab_ids).astype(f32)
    ratio = capped / softcap
    slopes = 1.0 - ratio * ratio
    logit_grad = ((weights / totals - onehot) * slopes).astype(bf16)

    contract = (((0,), (0,)), ((), ()))
    partial_hidden = lax.dot_general(table, logit_grad, contract, preferred_element_type=f32).astype(
        bf16
    )
    side = partial_hidden[:, :tokens].reshape(NZ, NX, high, tokens)

    def block_x(k):
        return lax.dynamic_slice(side, (0, (x + k) % NX, 0, 0), (NZ, 1, high, tokens))[:, 0]

    def absolute(value):
        shaped = value.reshape((4, 2) + value.shape[1:])
        picked = [lax.dynamic_index_in_dim(shaped, q ^ section, 0, False) for q in range(4)]
        return jnp.concatenate(picked)

    ordered = absolute(partial_hidden[:, tokens:].reshape(NZ, NX * 2, width, tokens)).reshape(
        NZ, NX, 2, width, tokens
    )

    def block_y(k):
        other = (y + k) % NY
        return lax.dynamic_slice(
            ordered, (0, 0, other // 2, 0, (other % 2) * lanes), (NZ, NX, 1, width, lanes)
        )[:, :, 0]

    sum_a = scatter_ring(block_x, x_up, x_down)
    sum_b = scatter_ring(block_y, y_up, y_down)
    sum_a = absolute(sum_a).astype(bf16).reshape(NZ, 2, width, tokens)
    sum_b = sum_b.astype(bf16)

    def block_y2(k):
        other = (y + k) % NY
        return lax.dynamic_slice(
            sum_a, (0, other // 2, 0, (other % 2) * lanes), (NZ, 1, width, lanes)
        )[:, 0]

    def block_x2(k):
        return lax.dynamic_slice(sum_b, (0, (x + k) % NX, 0, 0), (NZ, 1, width, lanes))[:, 0]

    sum_a = scatter_ring(block_y2, y_up, y_down).astype(bf16)
    sum_b = scatter_ring(block_x2, x_up, x_down).astype(bf16)
    last = lax.all_to_all(jnp.concatenate([sum_a, sum_b], axis=-1), "z", 0, 0)
    hidden_grad = jnp.sum(last.astype(f32), axis=0).astype(bf16).T

    window_grad = logit_grad[:window_rows]
    window_grad = jnp.where(yl == 0, window_grad, send(window_grad, swap_y))
    partial_grad = lax.dot_general(
        window_grad, states[: 2 * quarter], (((1,), (1,)), ((), ())), preferred_element_type=f32
    )
    grad_part = partial_grad[:, :quarter] + send(partial_grad[:, quarter:], swap_core)
    grad = grad_part + input_grad.astype(f32)
    new_first = beta_one * first_moment + (1.0 - beta_one) * grad
    new_second = beta_two * second_moment + (1.0 - beta_two) * grad * grad
    correct_one = 1.0 - beta_one**adam_step
    correct_two = 1.0 - beta_two**adam_step
    update = new_first / correct_one / (jnp.sqrt(new_second / correct_two) + epsilon)
    own_columns = embedding[:window_rows]
    new_part = (own_columns.astype(f32) - learn_rate * update).astype(bf16)
    new_pair = jnp.stack([new_part, send(new_part, swap_core)])
    far = send(new_part, swap_y)
    four = jnp.concatenate([new_pair, jnp.stack([far, send(far, swap_core)])])
    new_embedding = jnp.concatenate(
        [lax.dynamic_index_in_dim(four, q ^ section, 0, False) for q in range(4)], axis=1
    )
    blocks = exponents.shape[1]
    scaling = power_two(-exponents)
    shaped = new_part.astype(f32).reshape(window_rows, blocks, BLOCK) * scaling[:, :, None]
    scaled_table = jnp.clip(shaped, -448.0, 448.0).reshape(window_rows, quarter).astype(bf16)
    return (hidden_grad, new_embedding, new_first, new_second, scaled_table)


def solution(mesh):
    fine = Mesh(mesh.devices.reshape(2, 2, NZ, NX, 2), AXES)
    section, fsdp = ("yl", "c"), ("z", "x", "yh")
    placed = (
        P(section, fsdp),
        P(fsdp, section),
        P(section),
        P(fsdp, section),
        P(fsdp, section),
        P(fsdp, section),
        P(fsdp, section),
    )
    return jax.shard_map(
        local,
        mesh=fine,
        in_specs=placed,
        out_specs=(
            P(section, fsdp),
            P(fsdp, None),
            P(fsdp, section),
            P(fsdp, section),
            P(fsdp, section),
        ),
        check_vma=False,
    )
```

```python
import jax
import jax.numpy as jnp
from jax import lax
from jax.sharding import Mesh
from jax.sharding import PartitionSpec as P

BLOCK = 128
AXES = ("yl", "c", "z", "x", "yh")
NZ, NX, NY = 8, 4, 4

softcap = 30.0
learn_rate = 0.01
beta_one = 0.9
beta_two = 0.95
adam_step = 100.0
epsilon = 1e-08
bf16 = jnp.bfloat16
f32 = jnp.float32


def power_two(shifts):
    result = jnp.ones(shifts.shape, f32)
    for bit in range(4):
        factor = float(2**2**bit)
        result = result * jnp.where(shifts >> bit & 1 == 1, factor, 1.0).astype(f32)
    return result


def turn(axis, size, step):
    return axis, [(i, (i + step) % size) for i in range(size)]


def turn_y(step):
    place = lambda y: (y % 2) * 2 + y // 2
    return ("yl", "yh"), [(place(y), place((y + step) % NY)) for y in range(NY)]


def send(value, way):
    axis, pairs = way
    return lax.ppermute(value, axis, pairs)


def tie(value, *others):
    return lax.optimization_barrier((value, others))[0]


def local(hidden, embedding, targets, input_grad, first_moment, second_moment, exponents):
    yl, core, z, x, yh = (lax.axis_index(name) for name in AXES)
    section = yl * 2 + core
    fsdp = (z * NX + x) * 2 + yh
    y = yh * 2 + yl
    vocab_rows, quarter = embedding.shape
    rows = vocab_rows // 2
    tokens, width = hidden.shape
    window_rows = input_grad.shape[0]
    lanes = tokens // 2
    high = 2 * width
    swap_y = turn("yl", 2, 1)
    swap_core = turn("c", 2, 1)
    swap_far = turn("yh", 2, 1)
    swap_both = ("yl", "yh"), [(i, 3 - i) for i in range(NY)]
    x_up, x_down = turn("x", NX, 1), turn("x", NX, -1)
    z_up, z_down = turn("z", NZ, 1), turn("z", NZ, -1)
    y_up, y_down = turn_y(1), turn_y(-1)

    def pair_lanes(own, other):
        one = jnp.where(yl == 0, own, other)
        two = jnp.where(yl == 0, other, own)
        return jnp.concatenate(
            [one[..., :lanes], two[..., :lanes], one[..., lanes:], two[..., lanes:]], axis=-1
        )

    turned = hidden.T
    both = pair_lanes(turned, send(turned, swap_y))
    other_both = pair_lanes(send(turned, swap_far), send(turned, swap_both))
    goals = pair_lanes(targets, send(targets, swap_y))
    strip = jnp.concatenate(
        [jnp.where(yh == 0, both, other_both), jnp.where(yh == 0, other_both, both)], axis=0
    )

    away = (1 - yl) * rows
    part = lax.dynamic_slice(embedding, (away, 0), (rows, quarter))
    mine = lax.dynamic_slice(embedding, (yl * rows, 0), (rows, quarter))
    strip = tie(strip, part, mine, goals)
    far = send(tie(part, strip), swap_y)
    near = send(tie(mine, strip), swap_core)

    def relative(value):
        shaped = value.reshape((4, 2) + value.shape[1:])
        picked = [lax.dynamic_index_in_dim(shaped, q ^ section, 0, False) for q in range(4)]
        return jnp.concatenate(picked)

    strip_a, strip_b = strip[:, :tokens], strip[:, tokens:]
    arrived = [send(strip_a, turn("x", NX, step)) for step in (1, 3, 2)]
    across = jnp.zeros((NX, high, tokens), bf16)
    across = lax.dynamic_update_slice(across, strip_a[None], (x, 0, 0))
    for step, block in zip((1, 3, 2), arrived):
        across = lax.dynamic_update_slice(across, block[None], ((x - step) % NX, 0, 0))
    along = lax.all_to_all(jnp.broadcast_to(strip_b[None], (NZ, high, tokens)), "z", 0, 0)
    along = relative(tie(along, near, across))

    def cut_half(value):
        return value[: value.shape[0] // 2], value[value.shape[0] // 2 :]

    a1_low, a1_high = send(across, z_up), send(across, z_down)
    b_low, b_high = send(along, x_up), send(along, x_down)
    a2_low, a2_high = send(tie(a1_low, along), z_up), send(tie(a1_high, along), z_down)
    halves = cut_half(b_low)[0], cut_half(b_high)[1]
    a3_low, a3_high = send(a2_low, z_up), send(a2_high, z_down)
    b2_low = send(tie(halves[0], a2_low, a2_high), x_up)
    b2_high = send(tie(halves[1], a2_low, a2_high), x_down)
    a4_low = send(cut_half(a3_low)[0], z_up)
    a4_high = send(cut_half(a3_high)[1], z_down)
    far_core = send(tie(far, b2_low, b2_high), swap_core)
    table = mine, near, far, far_core

    states = jnp.zeros((NZ, NX, high, 2 * tokens), bf16)

    def put(states, value, offset, lead=0):
        place = ((z + offset) % NZ) ^ (2 * section)
        return lax.dynamic_update_slice(states, value[None], (place, lead, 0, 0))

    def put_x(states, value, offset, lead=0):
        return lax.dynamic_update_slice(
            states, value[:, None], (lead, (x + offset) % NX, 0, tokens)
        )

    states = put(states, across, 0)
    states = put_x(states, along, 0)
    for offset, low, upper in ((1, a1_low, a1_high), (2, a2_low, a2_high)):
        states = put(put(states, low, -offset), upper, offset)
    states = put_x(put_x(states, b_low, -1), b_high, 1)
    states = put(put(states, a3_low, -3), a3_high, 3)
    states = put_x(put_x(states, b2_low, 2), b2_high, 2, NZ // 2)
    states = put(put(states, a4_low, 4), a4_high, 4, NX // 2)
    states = states.reshape(4, quarter, 2 * tokens)

    raw_logits = sum(
        jnp.dot(slot, states[j], preferred_element_type=f32) for j, slot in enumerate(table)
    )
    capped = softcap * jnp.tanh(raw_logits / softcap)
    weights = jnp.exp(capped)
    ratio = capped / softcap
    slopes = 1.0 - ratio * ratio
    sums = jnp.sum(weights, axis=0)
    window_logits = raw_logits[:window_rows]
    peers = NZ * NX * NY
    shaped_sums = sums.reshape(-1, BLOCK)
    everyone = lax.all_to_all(
        jnp.broadcast_to(shaped_sums[None], (peers,) + shaped_sums.shape),
        ("yl", "z", "x", "yh"),
        0,
        0,
    )
    window_other = send(tie(window_logits, sums), swap_y)
    totals = jnp.sum(everyone, axis=0).reshape(1, -1)
    ids = fsdp * vocab_rows + yl * rows + lax.broadcasted_iota(jnp.int32, (rows, 1), 0)
    onehot = (goals[None, :] == ids).astype(f32)
    logit_grad = ((weights / totals - onehot) * slopes).astype(bf16)

    contract = (((0,), (0,)), ((), ()))

    pulled = jnp.stack(
        [
            lax.dot_general(slot, logit_grad, contract, preferred_element_type=f32).astype(bf16)
            for slot in table
        ]
    )
    side = pulled[:, :, :tokens].reshape(NZ, NX, high, tokens)
    front = pulled[:, :, tokens:].reshape(NZ, NX, 2, width, tokens)

    def block_x(k):
        return lax.dynamic_slice(side, (0, (x + k) % NX, 0, 0), (NZ, 1, high, tokens))[:, 0]

    def block_y(k):
        other = (y + k) % NY
        return lax.dynamic_slice(
            front, (0, 0, other // 2, 0, (other % 2) * lanes), (NZ, NX, 1, width, lanes)
        )[:, :, 0]

    def other_chip_order(value):
        return jnp.concatenate([value[NZ // 2 :], value[: NZ // 2]])

    class Ring:
        def __init__(self, block, up, down, axis, fix):
            self.block, self.up, self.down, self.axis, self.fix = block, up, down, axis, fix
            self.one, self.two, self.three = block(1), block(2), block(3)
            self.half = self.one.shape[axis] // 2
            first = self.join(self.low(self.two), self.high(self.one))
            second = self.join(self.high(self.two), self.low(self.three))
            self.from_low, self.from_high = send(first, up), send(second, down)

        def low(self, value):
            return lax.slice_in_dim(value, 0, self.half, axis=self.axis)

        def high(self, value):
            return lax.slice_in_dim(value, self.half, 2 * self.half, axis=self.axis)

        def join(self, *values):
            return jnp.concatenate(values, axis=self.axis)

        def finish(self, other, before):
            seen = other.from_low, other.from_high, before
            low, high = self.fix(self.from_low.astype(f32)), self.fix(self.from_high.astype(f32))
            next_up = (self.low(self.one).astype(f32) + self.low(low)).astype(bf16)
            next_down = (self.high(self.three).astype(f32) + self.low(high)).astype(bf16)
            last_low = self.fix(send(tie(next_up, *seen), self.up).astype(f32))
            last_high = self.fix(send(tie(next_down, *seen), self.down).astype(f32))
            own = self.block(0).astype(f32)
            return self.join(
                self.low(own) + self.high(high) + last_low,
                self.high(own) + self.high(low) + last_high,
            )

    ring_a = Ring(block_x, x_up, x_down, 0, lambda value: value)
    ring_b = Ring(block_y, y_up, y_down, 1, other_chip_order)
    window_logits = jnp.where(yl == 0, window_logits, window_other)
    window_logits = tie(window_logits, pulled)
    capped = softcap * jnp.tanh(window_logits / softcap)
    weights = jnp.exp(capped)
    ratio = capped / softcap
    ids = fsdp * vocab_rows + lax.broadcasted_iota(jnp.int32, (window_rows, 1), 0)
    onehot = (goals[None, :] == ids).astype(f32)
    window_grad = ((weights / totals - onehot) * (1.0 - ratio * ratio)).astype(bf16)
    partial_grad = [
        lax.dot_general(
            window_grad, states[j], (((1,), (1,)), ((), ())), preferred_element_type=f32
        )
        for j in range(2)
    ]
    grad_part = partial_grad[0] + send(partial_grad[1], swap_core)
    grad = grad_part + input_grad.astype(f32)
    new_first = beta_one * first_moment + (1.0 - beta_one) * grad
    new_second = beta_two * second_moment + (1.0 - beta_two) * grad * grad
    correct_one = 1.0 - beta_one**adam_step
    correct_two = 1.0 - beta_two**adam_step
    update = new_first / correct_one / (jnp.sqrt(new_second / correct_two) + epsilon)
    own_columns = embedding[:window_rows]
    new_part = (own_columns.astype(f32) - learn_rate * update).astype(bf16)
    sum_a = relative(ring_a.finish(ring_b, new_part)).astype(bf16).reshape(NZ, 2, width, tokens)
    sum_b = relative(ring_b.finish(ring_a, new_part)).astype(bf16)

    def block_y2(k):
        other = (y + k) % NY
        return lax.dynamic_slice(
            sum_a, (0, other // 2, 0, (other % 2) * lanes), (NZ, 1, width, lanes)
        )[:, 0]

    def block_x2(k):
        return lax.dynamic_slice(sum_b, (0, (x + k) % NX, 0, 0), (NZ, 1, width, lanes))[:, 0]

    def straight(block, way):
        return block(0).astype(f32) + sum(send(block(k), way(k)).astype(f32) for k in (2, 1, 3))

    sum_a, sum_b = tie(sum_a, sum_b), tie(sum_b, sum_a)
    sum_a = straight(block_y2, turn_y).astype(bf16)
    sum_b = straight(block_x2, lambda k: turn("x", NX, k)).astype(bf16)
    last = jnp.concatenate([sum_a, sum_b], axis=-1)
    spread = lax.all_to_all(last, "z", 0, 0)
    hidden_grad = jnp.sum(spread.astype(f32), axis=0).astype(bf16).T

    given = tie(new_part, last)
    far = send(given, swap_y)
    new_pair = jnp.stack([new_part, send(given, swap_core)])
    four = jnp.concatenate([new_pair, jnp.stack([far, send(far, swap_core)])])
    new_embedding = jnp.concatenate(
        [lax.dynamic_index_in_dim(four, q ^ section, 0, False) for q in range(4)], axis=1
    )
    blocks = exponents.shape[1]
    scaling = power_two(-exponents)
    shaped = new_part.astype(f32).reshape(window_rows, blocks, BLOCK) * scaling[:, :, None]
    scaled_table = jnp.clip(shaped, -448.0, 448.0).reshape(window_rows, quarter).astype(bf16)
    return (hidden_grad, new_embedding, new_first, new_second, scaled_table)


def solution(mesh):
    fine = Mesh(mesh.devices.reshape(2, 2, NZ, NX, 2), AXES)
    section, fsdp = ("yl", "c"), ("z", "x", "yh")
    placed = (
        P(section, fsdp),
        P(fsdp, section),
        P(section),
        P(fsdp, section),
        P(fsdp, section),
        P(fsdp, section),
        P(fsdp, section),
    )
    return jax.shard_map(
        local,
        mesh=fine,
        in_specs=placed,
        out_specs=(
            P(section, fsdp),
            P(fsdp, None),
            P(fsdp, section),
            P(fsdp, section),
            P(fsdp, section),
        ),
        check_vma=False,
    )
```

```python
import jax
import jax.numpy as jnp
from jax import lax
from jax.experimental import pallas as pl
from jax.experimental.pallas import tpu as pltpu
from jax.sharding import Mesh
from jax.sharding import PartitionSpec as P

BLOCK = 128
AXES = ("yl", "c", "z", "x", "yh")
NZ, NX, NY = 8, 4, 4
TILE = 256

softcap = 30.0
learn_rate = 0.01
beta_one = 0.9
beta_two = 0.95
adam_step = 100.0
epsilon = 1e-08
bf16 = jnp.bfloat16
f32 = jnp.float32


def power_two(shifts):
    result = jnp.ones(shifts.shape, f32)
    for bit in range(4):
        factor = float(2**2**bit)
        result = result * jnp.where(shifts >> bit & 1 == 1, factor, 1.0).astype(f32)
    return result


def turn(axis, size, step):
    return axis, [(i, (i + step) % size) for i in range(size)]


def turn_y(step):
    place = lambda y: (y % 2) * 2 + y // 2
    return ("yl", "yh"), [(place(y), place((y + step) % NY)) for y in range(NY)]


def send(value, way):
    axis, pairs = way
    return lax.ppermute(value, axis, pairs)


def logit_kernel(rows, own, near, far, far_core, states, raw, sums):
    step = pl.program_id(0)
    slots = own, near, far, far_core
    total = sum(
        jnp.dot(slot[...], states[j], preferred_element_type=f32) for j, slot in enumerate(slots)
    )
    raw[...] = total
    weights = jnp.exp(softcap * jnp.tanh(total / softcap))
    row = step * TILE + lax.broadcasted_iota(jnp.int32, (TILE, 1), 0)
    part = jnp.sum(jnp.where(row < rows, weights, 0.0), axis=0, keepdims=True)

    @pl.when(step == 0)
    def _():
        sums[...] = part

    @pl.when(step > 0)
    def _():
        sums[...] += part


def logits_of(table, states):
    rows, quarter = table[0].shape
    tokens = states.shape[2]
    work = 2 * rows * 4 * quarter * tokens
    return pl.pallas_call(
        lambda *refs: logit_kernel(rows, *refs),
        grid=(pl.cdiv(rows, TILE),),
        in_specs=[pl.BlockSpec((TILE, quarter), lambda i: (i, 0))] * 4
        + [pl.BlockSpec(states.shape, lambda i: (0, 0, 0))],
        out_specs=[
            pl.BlockSpec((TILE, tokens), lambda i: (i, 0)),
            pl.BlockSpec((1, tokens), lambda i: (0, 0)),
        ],
        out_shape=[
            jax.ShapeDtypeStruct((rows, tokens), f32),
            jax.ShapeDtypeStruct((1, tokens), f32),
        ],
        compiler_params=pltpu.CompilerParams(
            dimension_semantics=("arbitrary",), vmem_limit_bytes=32 * 2**20
        ),
        cost_estimate=pl.CostEstimate(
            flops=work, bytes_accessed=16 * 2**20, transcendentals=2 * rows * tokens
        ),
    )(*table, states)


def tie(value, *others):
    return lax.optimization_barrier((value, others))[0]


def local(hidden, embedding, targets, input_grad, first_moment, second_moment, exponents):
    yl, core, z, x, yh = (lax.axis_index(name) for name in AXES)
    section = yl * 2 + core
    fsdp = (z * NX + x) * 2 + yh
    y = yh * 2 + yl
    vocab_rows, quarter = embedding.shape
    rows = vocab_rows // 2
    tokens, width = hidden.shape
    window_rows = input_grad.shape[0]
    lanes = tokens // 2
    high = 2 * width
    swap_y = turn("yl", 2, 1)
    swap_core = turn("c", 2, 1)
    swap_far = turn("yh", 2, 1)
    swap_both = ("yl", "yh"), [(i, 3 - i) for i in range(NY)]
    x_up, x_down = turn("x", NX, 1), turn("x", NX, -1)
    z_up, z_down = turn("z", NZ, 1), turn("z", NZ, -1)
    y_up, y_down = turn_y(1), turn_y(-1)

    def pair_lanes(own, other):
        one = jnp.where(yl == 0, own, other)
        two = jnp.where(yl == 0, other, own)
        return jnp.concatenate(
            [one[..., :lanes], two[..., :lanes], one[..., lanes:], two[..., lanes:]], axis=-1
        )

    turned = hidden.T
    both = pair_lanes(turned, send(turned, swap_y))
    other_both = pair_lanes(send(turned, swap_far), send(turned, swap_both))
    goals = pair_lanes(targets, send(targets, swap_y))
    strip = jnp.concatenate(
        [jnp.where(yh == 0, both, other_both), jnp.where(yh == 0, other_both, both)], axis=0
    )

    away = (1 - yl) * rows
    part = lax.dynamic_slice(embedding, (away, 0), (rows, quarter))
    mine = lax.dynamic_slice(embedding, (yl * rows, 0), (rows, quarter))
    strip = tie(strip, part, mine, goals)
    far = send(tie(part, strip), swap_y)
    near = send(tie(mine, strip), swap_core)

    def relative(value):
        shaped = value.reshape((4, 2) + value.shape[1:])
        picked = [lax.dynamic_index_in_dim(shaped, q ^ section, 0, False) for q in range(4)]
        return jnp.concatenate(picked)

    strip_a, strip_b = strip[:, :tokens], strip[:, tokens:]
    arrived = [send(strip_a, turn("x", NX, step)) for step in (1, 3, 2)]
    across = jnp.zeros((NX, high, tokens), bf16)
    across = lax.dynamic_update_slice(across, strip_a[None], (x, 0, 0))
    for step, block in zip((1, 3, 2), arrived):
        across = lax.dynamic_update_slice(across, block[None], ((x - step) % NX, 0, 0))
    along = lax.all_to_all(jnp.broadcast_to(strip_b[None], (NZ, high, tokens)), "z", 0, 0)
    along = relative(tie(along, near, across))

    def cut_half(value):
        return value[: value.shape[0] // 2], value[value.shape[0] // 2 :]

    a1_low, a1_high = send(across, z_up), send(across, z_down)
    b_low, b_high = send(along, x_up), send(along, x_down)
    a2_low, a2_high = send(tie(a1_low, along), z_up), send(tie(a1_high, along), z_down)
    halves = cut_half(b_low)[0], cut_half(b_high)[1]
    a3_low, a3_high = send(a2_low, z_up), send(a2_high, z_down)
    b2_low = send(tie(halves[0], a3_low, a3_high), x_up)
    b2_high = send(tie(halves[1], a3_low, a3_high), x_down)
    a4_low = send(cut_half(a3_low)[0], z_up)
    a4_high = send(cut_half(a3_high)[1], z_down)
    far_core = send(tie(far, b2_low, b2_high, a4_low, a4_high), swap_core)
    table = mine, near, far, far_core

    states = jnp.zeros((NZ, NX, high, 2 * tokens), bf16)

    def put(states, value, offset, lead=0):
        place = ((z + offset) % NZ) ^ (2 * section)
        return lax.dynamic_update_slice(states, value[None], (place, lead, 0, 0))

    def put_x(states, value, offset, lead=0):
        return lax.dynamic_update_slice(
            states, value[:, None], (lead, (x + offset) % NX, 0, tokens)
        )

    states = put(states, across, 0)
    states = put_x(states, along, 0)
    for offset, low, upper in ((1, a1_low, a1_high), (2, a2_low, a2_high)):
        states = put(put(states, low, -offset), upper, offset)
    states = put_x(put_x(states, b_low, -1), b_high, 1)
    states = put(put(states, a3_low, -3), a3_high, 3)
    states = put_x(put_x(states, b2_low, 2), b2_high, 2, NZ // 2)
    states = put(put(states, a4_low, 4), a4_high, 4, NX // 2)
    states = states.reshape(4, quarter, 2 * tokens)

    raw_logits, sums = logits_of(table, states)
    capped = softcap * jnp.tanh(raw_logits / softcap)
    weights = jnp.exp(capped)
    ratio = capped / softcap
    slopes = 1.0 - ratio * ratio
    window_logits = raw_logits[:window_rows]
    peers = NZ * NX * NY
    shaped_sums = sums.reshape(-1, BLOCK)
    everyone = lax.all_to_all(
        jnp.broadcast_to(shaped_sums[None], (peers,) + shaped_sums.shape),
        ("yl", "z", "x", "yh"),
        0,
        0,
    )
    window_other = send(tie(window_logits, sums), swap_y)
    totals = jnp.sum(everyone, axis=0).reshape(1, -1)
    ids = fsdp * vocab_rows + yl * rows + lax.broadcasted_iota(jnp.int32, (rows, 1), 0)
    onehot = (goals[None, :] == ids).astype(f32)
    logit_grad = ((weights / totals - onehot) * slopes).astype(bf16)

    contract = (((0,), (0,)), ((), ()))

    pulled = jnp.stack(
        [
            lax.dot_general(slot, logit_grad, contract, preferred_element_type=f32).astype(bf16)
            for slot in table
        ]
    )
    side = pulled[:, :, :tokens].reshape(NZ, NX, high, tokens)
    front = pulled[:, :, tokens:].reshape(NZ, NX, 2, width, tokens)

    def block_x(k):
        return lax.dynamic_slice(side, (0, (x + k) % NX, 0, 0), (NZ, 1, high, tokens))[:, 0]

    def block_y(k):
        other = (y + k) % NY
        return lax.dynamic_slice(
            front, (0, 0, other // 2, 0, (other % 2) * lanes), (NZ, NX, 1, width, lanes)
        )[:, :, 0]

    def other_chip_order(value):
        return jnp.concatenate([value[NZ // 2 :], value[: NZ // 2]])

    class Ring:
        def __init__(self, block, up, down, axis, fix):
            self.block, self.up, self.down, self.axis, self.fix = block, up, down, axis, fix
            self.one, self.two, self.three = block(1), block(2), block(3)
            self.half = self.one.shape[axis] // 2
            first = self.join(self.low(self.two), self.high(self.one))
            second = self.join(self.high(self.two), self.low(self.three))
            self.from_low, self.from_high = send(first, up), send(second, down)

        def low(self, value):
            return lax.slice_in_dim(value, 0, self.half, axis=self.axis)

        def high(self, value):
            return lax.slice_in_dim(value, self.half, 2 * self.half, axis=self.axis)

        def join(self, *values):
            return jnp.concatenate(values, axis=self.axis)

        def finish(self, *seen):
            low, high = self.fix(self.from_low.astype(f32)), self.fix(self.from_high.astype(f32))
            next_up = (self.low(self.one).astype(f32) + self.low(low)).astype(bf16)
            next_down = (self.high(self.three).astype(f32) + self.low(high)).astype(bf16)
            self.next = next_up, next_down
            last_low = self.fix(send(tie(next_up, *seen), self.up).astype(f32))
            last_high = self.fix(send(tie(next_down, *seen), self.down).astype(f32))
            own = self.block(0).astype(f32)
            return self.join(
                self.low(own) + self.high(high) + last_low,
                self.high(own) + self.high(low) + last_high,
            )

    ring_a = Ring(block_x, x_up, x_down, 0, lambda value: value)
    ring_b = Ring(block_y, y_up, y_down, 1, other_chip_order)
    window_logits = jnp.where(yl == 0, window_logits, window_other)
    window_logits = tie(window_logits, pulled)
    capped = softcap * jnp.tanh(window_logits / softcap)
    weights = jnp.exp(capped)
    ratio = capped / softcap
    ids = fsdp * vocab_rows + lax.broadcasted_iota(jnp.int32, (window_rows, 1), 0)
    onehot = (goals[None, :] == ids).astype(f32)
    window_grad = ((weights / totals - onehot) * (1.0 - ratio * ratio)).astype(bf16)
    partial_grad = [
        lax.dot_general(
            window_grad, states[j], (((1,), (1,)), ((), ())), preferred_element_type=f32
        )
        for j in range(2)
    ]
    grad_part = partial_grad[0] + send(partial_grad[1], swap_core)
    grad = grad_part + input_grad.astype(f32)
    new_first = beta_one * first_moment + (1.0 - beta_one) * grad
    new_second = beta_two * second_moment + (1.0 - beta_two) * grad * grad
    correct_one = 1.0 - beta_one**adam_step
    correct_two = 1.0 - beta_two**adam_step
    update = new_first / correct_one / (jnp.sqrt(new_second / correct_two) + epsilon)
    own_columns = embedding[:window_rows]
    new_part = (own_columns.astype(f32) - learn_rate * update).astype(bf16)
    sum_a = relative(ring_a.finish()).astype(bf16).reshape(NZ, 2, width, tokens)
    last_step = ring_a.next
    sum_b = relative(ring_b.finish(new_part, last_step)).astype(bf16)

    def block_y2(k):
        other = (y + k) % NY
        return lax.dynamic_slice(
            sum_a, (0, other // 2, 0, (other % 2) * lanes), (NZ, 1, width, lanes)
        )[:, 0]

    def block_x2(k):
        return lax.dynamic_slice(sum_b, (0, (x + k) % NX, 0, 0), (NZ, 1, width, lanes))[:, 0]

    def straight(block, way):
        return block(0).astype(f32) + sum(send(block(k), way(k)).astype(f32) for k in (2, 1, 3))

    sum_a, sum_b = tie(sum_a, sum_b), tie(sum_b, sum_a)
    sum_a = straight(block_y2, turn_y).astype(bf16)
    sum_b = straight(block_x2, lambda k: turn("x", NX, k)).astype(bf16)
    last = jnp.concatenate([sum_a, sum_b], axis=-1)
    spread = lax.all_to_all(last, "z", 0, 0)
    hidden_grad = jnp.sum(spread.astype(f32), axis=0).astype(bf16).T

    given = tie(new_part, last)
    far = send(given, swap_y)
    new_pair = jnp.stack([new_part, send(given, swap_core)])
    four = jnp.concatenate([new_pair, jnp.stack([far, send(far, swap_core)])])
    new_embedding = jnp.concatenate(
        [lax.dynamic_index_in_dim(four, q ^ section, 0, False) for q in range(4)], axis=1
    )
    blocks = exponents.shape[1]
    scaling = power_two(-exponents)
    shaped = new_part.astype(f32).reshape(window_rows, blocks, BLOCK) * scaling[:, :, None]
    scaled_table = jnp.clip(shaped, -448.0, 448.0).reshape(window_rows, quarter).astype(bf16)
    return (hidden_grad, new_embedding, new_first, new_second, scaled_table)


def solution(mesh):
    fine = Mesh(mesh.devices.reshape(2, 2, NZ, NX, 2), AXES)
    section, fsdp = ("yl", "c"), ("z", "x", "yh")
    placed = (
        P(section, fsdp),
        P(fsdp, section),
        P(section),
        P(fsdp, section),
        P(fsdp, section),
        P(fsdp, section),
        P(fsdp, section),
    )
    return jax.shard_map(
        local,
        mesh=fine,
        in_specs=placed,
        out_specs=(
            P(section, fsdp),
            P(fsdp, None),
            P(fsdp, section),
            P(fsdp, section),
            P(fsdp, section),
        ),
        check_vma=False,
    )
```

```python
import jax
import jax.numpy as jnp
from jax import lax
from jax.experimental import pallas as pl
from jax.experimental.pallas import tpu as pltpu
from jax.sharding import Mesh
from jax.sharding import PartitionSpec as P

BLOCK = 128
AXES = ("yl", "c", "z", "x", "yh")
NZ, NX, NY = 8, 4, 4
TILE = 256
SLAB = 384

softcap = 30.0
learn_rate = 0.01
beta_one = 0.9
beta_two = 0.95
adam_step = 100.0
epsilon = 1e-08
bf16 = jnp.bfloat16
f32 = jnp.float32


def power_two(shifts):
    result = jnp.ones(shifts.shape, f32)
    for bit in range(4):
        factor = float(2**2**bit)
        result = result * jnp.where(shifts >> bit & 1 == 1, factor, 1.0).astype(f32)
    return result


def turn(axis, size, step):
    return axis, [(i, (i + step) % size) for i in range(size)]


def turn_y(step):
    place = lambda y: (y % 2) * 2 + y // 2
    return ("yl", "yh"), [(place(y), place((y + step) % NY)) for y in range(NY)]


def send(value, way):
    axis, pairs = way
    return lax.ppermute(value, axis, pairs)


def logit_kernel(rows, own, near, far, far_core, states, raw, sums):
    step = pl.program_id(0)
    slots = own, near, far, far_core
    total = sum(
        jnp.dot(slot[...], states[j], preferred_element_type=f32) for j, slot in enumerate(slots)
    )
    raw[...] = total
    weights = jnp.exp(softcap * jnp.tanh(total / softcap))
    row = step * TILE + lax.broadcasted_iota(jnp.int32, (TILE, 1), 0)
    part = jnp.sum(jnp.where(row < rows, weights, 0.0), axis=0, keepdims=True)

    @pl.when(step == 0)
    def _():
        sums[...] = part

    @pl.when(step > 0)
    def _():
        sums[...] += part


def logits_of(table, states):
    rows, quarter = table[0].shape
    tokens = states.shape[2]
    work = 2 * rows * 4 * quarter * tokens
    return pl.pallas_call(
        lambda *refs: logit_kernel(rows, *refs),
        grid=(pl.cdiv(rows, TILE),),
        in_specs=[pl.BlockSpec((TILE, quarter), lambda i: (i, 0))] * 4
        + [pl.BlockSpec(states.shape, lambda i: (0, 0, 0))],
        out_specs=[
            pl.BlockSpec((TILE, tokens), lambda i: (i, 0)),
            pl.BlockSpec((1, tokens), lambda i: (0, 0)),
        ],
        out_shape=[
            jax.ShapeDtypeStruct((rows, tokens), f32),
            jax.ShapeDtypeStruct((1, tokens), f32),
        ],
        compiler_params=pltpu.CompilerParams(
            dimension_semantics=("arbitrary",), vmem_limit_bytes=32 * 2**20
        ),
        cost_estimate=pl.CostEstimate(
            flops=work, bytes_accessed=16 * 2**20, transcendentals=2 * rows * tokens
        ),
    )(*table, states)


def pull_kernel(own, near, far, far_core, grads, out):
    contract = (((0,), (0,)), ((), ()))
    for j, slot in enumerate((own, near, far, far_core)):
        out[j] = lax.dot_general(
            slot[...], grads[...], contract, preferred_element_type=f32
        ).astype(bf16)


def pull_back(table, grads):
    rows, quarter = table[0].shape
    tokens = grads.shape[1]
    return pl.pallas_call(
        pull_kernel,
        grid=(quarter // SLAB,),
        in_specs=[pl.BlockSpec((rows, SLAB), lambda i: (0, i))] * 4
        + [pl.BlockSpec((rows, tokens), lambda i: (0, 0))],
        out_specs=pl.BlockSpec((4, SLAB, tokens), lambda i: (0, i, 0)),
        out_shape=jax.ShapeDtypeStruct((4, quarter, tokens), bf16),
        compiler_params=pltpu.CompilerParams(
            dimension_semantics=("arbitrary",), vmem_limit_bytes=32 * 2**20
        ),
        cost_estimate=pl.CostEstimate(
            flops=8 * rows * quarter * tokens, bytes_accessed=15 * 2**20, transcendentals=0
        ),
    )(*table, grads)


def tie(value, *others):
    return lax.optimization_barrier((value, others))[0]


def local(hidden, embedding, targets, input_grad, first_moment, second_moment, exponents):
    yl, core, z, x, yh = (lax.axis_index(name) for name in AXES)
    section = yl * 2 + core
    fsdp = (z * NX + x) * 2 + yh
    y = yh * 2 + yl
    vocab_rows, quarter = embedding.shape
    rows = vocab_rows // 2
    tokens, width = hidden.shape
    window_rows = input_grad.shape[0]
    lanes = tokens // 2
    high = 2 * width
    swap_y = turn("yl", 2, 1)
    swap_core = turn("c", 2, 1)
    swap_far = turn("yh", 2, 1)
    swap_both = ("yl", "yh"), [(i, 3 - i) for i in range(NY)]
    x_up, x_down = turn("x", NX, 1), turn("x", NX, -1)
    z_up, z_down = turn("z", NZ, 1), turn("z", NZ, -1)
    y_up, y_down = turn_y(1), turn_y(-1)

    def pair_lanes(own, other):
        one = jnp.where(yl == 0, own, other)
        two = jnp.where(yl == 0, other, own)
        return jnp.concatenate(
            [one[..., :lanes], two[..., :lanes], one[..., lanes:], two[..., lanes:]], axis=-1
        )

    turned = hidden.T
    both = pair_lanes(turned, send(turned, swap_y))
    other_both = pair_lanes(send(turned, swap_far), send(turned, swap_both))
    goals = pair_lanes(targets, send(targets, swap_y))
    strip = jnp.concatenate(
        [jnp.where(yh == 0, both, other_both), jnp.where(yh == 0, other_both, both)], axis=0
    )

    away = (1 - yl) * rows
    part = lax.dynamic_slice(embedding, (away, 0), (rows, quarter))
    mine = lax.dynamic_slice(embedding, (yl * rows, 0), (rows, quarter))
    strip = tie(strip, part, mine, goals)
    far = send(tie(part, strip), swap_y)
    near = send(tie(mine, strip), swap_core)

    def relative(value):
        shaped = value.reshape((4, 2) + value.shape[1:])
        picked = [lax.dynamic_index_in_dim(shaped, q ^ section, 0, False) for q in range(4)]
        return jnp.concatenate(picked)

    strip_a, strip_b = strip[:, :tokens], strip[:, tokens:]
    arrived = [send(strip_a, turn("x", NX, step)) for step in (1, 3, 2)]
    across = jnp.zeros((NX, high, tokens), bf16)
    across = lax.dynamic_update_slice(across, strip_a[None], (x, 0, 0))
    for step, block in zip((1, 3, 2), arrived):
        across = lax.dynamic_update_slice(across, block[None], ((x - step) % NX, 0, 0))
    along = lax.all_to_all(jnp.broadcast_to(strip_b[None], (NZ, high, tokens)), "z", 0, 0)
    along = relative(tie(along, near, across))

    def cut_half(value):
        return value[: value.shape[0] // 2], value[value.shape[0] // 2 :]

    a1_low, a1_high = send(across, z_up), send(across, z_down)
    b_low, b_high = send(along, x_up), send(along, x_down)
    a2_low, a2_high = send(tie(a1_low, along), z_up), send(tie(a1_high, along), z_down)
    halves = cut_half(b_low)[0], cut_half(b_high)[1]
    a3_low, a3_high = send(a2_low, z_up), send(a2_high, z_down)
    b2_low = send(tie(halves[0], a3_low, a3_high), x_up)
    b2_high = send(tie(halves[1], a3_low, a3_high), x_down)
    a4_low = send(cut_half(a3_low)[0], z_up)
    a4_high = send(cut_half(a3_high)[1], z_down)
    far_core = send(tie(far, b2_low, b2_high, a4_low, a4_high), swap_core)
    table = mine, near, far, far_core

    states = jnp.zeros((NZ, NX, high, 2 * tokens), bf16)

    def put(states, value, offset, lead=0):
        place = ((z + offset) % NZ) ^ (2 * section)
        return lax.dynamic_update_slice(states, value[None], (place, lead, 0, 0))

    def put_x(states, value, offset, lead=0):
        return lax.dynamic_update_slice(
            states, value[:, None], (lead, (x + offset) % NX, 0, tokens)
        )

    states = put(states, across, 0)
    states = put_x(states, along, 0)
    for offset, low, upper in ((1, a1_low, a1_high), (2, a2_low, a2_high)):
        states = put(put(states, low, -offset), upper, offset)
    states = put_x(put_x(states, b_low, -1), b_high, 1)
    states = put(put(states, a3_low, -3), a3_high, 3)
    states = put_x(put_x(states, b2_low, 2), b2_high, 2, NZ // 2)
    states = put(put(states, a4_low, 4), a4_high, 4, NX // 2)
    states = states.reshape(4, quarter, 2 * tokens)

    raw_logits, sums = logits_of(table, states)
    capped = softcap * jnp.tanh(raw_logits / softcap)
    weights = jnp.exp(capped)
    ratio = capped / softcap
    slopes = 1.0 - ratio * ratio
    window_logits = raw_logits[:window_rows]
    peers = NZ * NX * NY
    shaped_sums = sums.reshape(-1, BLOCK)
    everyone = lax.all_to_all(
        jnp.broadcast_to(shaped_sums[None], (peers,) + shaped_sums.shape),
        ("yl", "z", "x", "yh"),
        0,
        0,
    )
    window_other = send(tie(window_logits, sums), swap_y)
    totals = jnp.sum(everyone, axis=0).reshape(1, -1)
    ids = fsdp * vocab_rows + yl * rows + lax.broadcasted_iota(jnp.int32, (rows, 1), 0)
    onehot = (goals[None, :] == ids).astype(f32)
    logit_grad = ((weights / totals - onehot) * slopes).astype(bf16)

    pulled = pull_back(table, logit_grad)
    side = pulled[:, :, :tokens].reshape(NZ, NX, high, tokens)
    front = pulled[:, :, tokens:].reshape(NZ, NX, 2, width, tokens)

    def block_x(k):
        return lax.dynamic_slice(side, (0, (x + k) % NX, 0, 0), (NZ, 1, high, tokens))[:, 0]

    def block_y(k):
        other = (y + k) % NY
        return lax.dynamic_slice(
            front, (0, 0, other // 2, 0, (other % 2) * lanes), (NZ, NX, 1, width, lanes)
        )[:, :, 0]

    def other_chip_order(value):
        return jnp.concatenate([value[NZ // 2 :], value[: NZ // 2]])

    class Ring:
        def __init__(self, block, up, down, axis, fix):
            self.block, self.up, self.down, self.axis, self.fix = block, up, down, axis, fix
            self.one, self.two, self.three = block(1), block(2), block(3)
            self.half = self.one.shape[axis] // 2
            first = self.join(self.low(self.two), self.high(self.one))
            second = self.join(self.high(self.two), self.low(self.three))
            self.from_low, self.from_high = send(first, up), send(second, down)

        def low(self, value):
            return lax.slice_in_dim(value, 0, self.half, axis=self.axis)

        def high(self, value):
            return lax.slice_in_dim(value, self.half, 2 * self.half, axis=self.axis)

        def join(self, *values):
            return jnp.concatenate(values, axis=self.axis)

        def finish(self, *seen):
            low, high = self.fix(self.from_low.astype(f32)), self.fix(self.from_high.astype(f32))
            next_up = (self.low(self.one).astype(f32) + self.low(low)).astype(bf16)
            next_down = (self.high(self.three).astype(f32) + self.low(high)).astype(bf16)
            self.next = next_up, next_down
            last_low = self.fix(send(tie(next_up, *seen), self.up).astype(f32))
            last_high = self.fix(send(tie(next_down, *seen), self.down).astype(f32))
            own = self.block(0).astype(f32)
            return self.join(
                self.low(own) + self.high(high) + last_low,
                self.high(own) + self.high(low) + last_high,
            )

    ring_a = Ring(block_x, x_up, x_down, 0, lambda value: value)
    ring_b = Ring(block_y, y_up, y_down, 1, other_chip_order)
    window_logits = jnp.where(yl == 0, window_logits, window_other)
    window_logits = tie(window_logits, pulled)
    capped = softcap * jnp.tanh(window_logits / softcap)
    weights = jnp.exp(capped)
    ratio = capped / softcap
    ids = fsdp * vocab_rows + lax.broadcasted_iota(jnp.int32, (window_rows, 1), 0)
    onehot = (goals[None, :] == ids).astype(f32)
    window_grad = ((weights / totals - onehot) * (1.0 - ratio * ratio)).astype(bf16)
    partial_grad = [
        lax.dot_general(
            window_grad, states[j], (((1,), (1,)), ((), ())), preferred_element_type=f32
        )
        for j in range(2)
    ]
    grad_part = partial_grad[0] + send(partial_grad[1], swap_core)
    grad = grad_part + input_grad.astype(f32)
    new_first = beta_one * first_moment + (1.0 - beta_one) * grad
    new_second = beta_two * second_moment + (1.0 - beta_two) * grad * grad
    correct_one = 1.0 - beta_one**adam_step
    correct_two = 1.0 - beta_two**adam_step
    update = new_first / correct_one / (jnp.sqrt(new_second / correct_two) + epsilon)
    own_columns = embedding[:window_rows]
    new_part = (own_columns.astype(f32) - learn_rate * update).astype(bf16)
    sum_a = relative(ring_a.finish()).astype(bf16).reshape(NZ, 2, width, tokens)
    last_step = ring_a.next
    sum_b = relative(ring_b.finish(new_part, last_step)).astype(bf16)

    def block_y2(k):
        other = (y + k) % NY
        return lax.dynamic_slice(
            sum_a, (0, other // 2, 0, (other % 2) * lanes), (NZ, 1, width, lanes)
        )[:, 0]

    def block_x2(k):
        return lax.dynamic_slice(sum_b, (0, (x + k) % NX, 0, 0), (NZ, 1, width, lanes))[:, 0]

    def straight(block, way):
        return block(0).astype(f32) + sum(send(block(k), way(k)).astype(f32) for k in (2, 1, 3))

    sum_a, sum_b = tie(sum_a, sum_b), tie(sum_b, sum_a)
    sum_a = straight(block_y2, turn_y).astype(bf16)
    sum_b = straight(block_x2, lambda k: turn("x", NX, k)).astype(bf16)
    last = jnp.concatenate([sum_a, sum_b], axis=-1)
    spread = lax.all_to_all(last, "z", 0, 0)
    hidden_grad = jnp.sum(spread.astype(f32), axis=0).astype(bf16).T

    given = tie(new_part, last)
    far = send(given, swap_y)
    new_pair = jnp.stack([new_part, send(given, swap_core)])
    four = jnp.concatenate([new_pair, jnp.stack([far, send(far, swap_core)])])
    new_embedding = jnp.concatenate(
        [lax.dynamic_index_in_dim(four, q ^ section, 0, False) for q in range(4)], axis=1
    )
    blocks = exponents.shape[1]
    scaling = power_two(-exponents)
    shaped = new_part.astype(f32).reshape(window_rows, blocks, BLOCK) * scaling[:, :, None]
    scaled_table = jnp.clip(shaped, -448.0, 448.0).reshape(window_rows, quarter).astype(bf16)
    return (hidden_grad, new_embedding, new_first, new_second, scaled_table)


def solution(mesh):
    fine = Mesh(mesh.devices.reshape(2, 2, NZ, NX, 2), AXES)
    section, fsdp = ("yl", "c"), ("z", "x", "yh")
    placed = (
        P(section, fsdp),
        P(fsdp, section),
        P(section),
        P(fsdp, section),
        P(fsdp, section),
        P(fsdp, section),
        P(fsdp, section),
    )
    return jax.shard_map(
        local,
        mesh=fine,
        in_specs=placed,
        out_specs=(
            P(section, fsdp),
            P(fsdp, None),
            P(fsdp, section),
            P(fsdp, section),
            P(fsdp, section),
        ),
        check_vma=False,
    )
```
